256 devices in a mesh: theta: 8 (over z_hi, core), phi: 4 (over y), box: 8 (over z_lo, x).
Axes of the slice: x: 4, y: 4, z: 8 (z_hi: 4, z_lo: 2; z = z_hi * 2 + z_lo), core: 2. Of those that a mesh axis runs over, the one named last changes fastest.
Arguments:
- pattern: float32 [2, 64, 1024, 2048], P(None, 'box', 'theta', 'phi'), may hold values from -6 to 6
- legendre: bfloat16 [4, 128, 512, 512], P('phi', 'theta'), may hold values from -0.005859375 to 0.005859375
- degree: int32 [64], P('box'), may hold values from 256 to 512, as said below
- owner: int32 [64], replicated, may hold values from 0 to 63, as said below
Outputs:
- harmonics: bfloat16 [4, 64, 512, 512], P(None, 'box', 'theta', 'phi')
The draws below stay inside these ranges and needn't reach their ends.
Inputs may be any that keep to these rules, and one draw needn't show every extreme that they name: Some box has degree 512. owner is a permutation of the box numbers; of the 8 boxes b with the same b // 8, exactly 1 have owner[b] // 8 equal to each value 0 to 7.
All inputs are finite; a program needn't handle non-finite values.
Results may differ from the reference program's by a relative error of at most 0.0049.
Values may be sent and summed in bfloat16 or wider, within the bound.
A program may use at most 128 MiB of HBM per device.

```python
import jax
import jax.numpy as jnp
from jax import lax

NT = 1024
NP = 2048
L = 512
B_DEV = 8
K = 512
NH = 512
PHI_GROUPS = 4
KP = 128
BOX_GROUPS = 8
SEND_EACH = 1
BOXES = 64


def draw_owner(key, part):
    key = jax.random.fold_in(key, 11)
    source_key, target_key = jax.random.split(key)

    def one_permutation(single_key):
        return jax.random.permutation(single_key, B_DEV).astype(jnp.int32)
    source_rank = jax.vmap(one_permutation)(jax.random.split(source_key, BOX_GROUPS))
    target_slots = jax.vmap(one_permutation)(jax.random.split(target_key, BOX_GROUPS))
    source_ids = jnp.broadcast_to(jnp.arange(BOX_GROUPS, dtype=jnp.int32)[:, None], (BOX_GROUPS, B_DEV))
    target = source_rank // SEND_EACH
    within = source_rank % SEND_EACH
    slot_place = target_slots[target, source_ids * SEND_EACH + within]
    return (target * B_DEV + slot_place).reshape(-1).astype(jnp.int32)


def draw_degree(key, part):
    key = jax.random.fold_in(key, 23)
    value_key, spot_key = jax.random.split(key)
    values = jax.random.randint(value_key, (BOXES,), L // 2, L + 1).astype(jnp.int32)
    spot_index = jax.random.randint(spot_key, (), 0, BOXES)
    return values.at[spot_index].set(L).astype(jnp.int32)


def block_scale(own_key, shape, cuts, low, top_value):
    loudness = 1.0
    for dim, parts in cuts:
        draws = jax.random.uniform(jax.random.fold_in(jax.random.fold_in(own_key, 6), dim), (parts,), jnp.float32, low / len(cuts), top_value / len(cuts))
        loudness = loudness * jnp.repeat(jnp.exp(draws), shape[dim] // parts).reshape((-1,) + (1,) * (len(shape) - 1 - dim))
    return loudness


def gaussian(key, dims, deviation, bound, cuts=(), kind=jnp.bfloat16):
    values = deviation * jax.random.normal(key, dims, jnp.float32)
    if cuts:
        values = values * block_scale(key, dims, cuts, -0.22, 0.18)
    return jnp.clip(values, -bound, bound).astype(kind)


def setup_inputs(seed: int = 0) -> dict:
    arg_keys = jax.random.split(jax.random.key(seed), 5)
    pattern = gaussian(arg_keys[0], (2, BOXES, NT, NP), 1.0, 6.0, ((1, 8), (2, 8), (3, 4)), jnp.float32)
    legendre = gaussian(arg_keys[1], (PHI_GROUPS, KP, NH, L), (NT * NP // 2) ** -0.5, 0.005859375, ((0, 4), (1, 8)))
    degree = draw_degree(jax.random.fold_in(arg_keys[4], 71), 0)
    owner = draw_owner(jax.random.fold_in(arg_keys[4], 71), 0)
    return dict(pattern=pattern, legendre=legendre, degree=degree, owner=owner)


def reference(pattern, legendre, degree, owner):
    fft_real = jnp.fft.rfft(pattern[0], axis=-1)[:, :, :K]
    fft_imag = jnp.fft.rfft(pattern[1], axis=-1)[:, :, :K]
    spectrum = jnp.stack([fft_real.real, fft_imag.real, -fft_real.imag, -fft_imag.imag]).astype(jnp.float32)
    north_rows = spectrum[:, :, :NH]
    south_rows = spectrum[:, :, NH:][:, :, ::-1]
    even_part = (north_rows + south_rows).astype(jnp.bfloat16)
    odd_part = (north_rows - south_rows).astype(jnp.bfloat16)
    even_orders = jnp.moveaxis(even_part, 3, 0).reshape(K, 4 * BOXES, NH)
    odd_orders = jnp.moveaxis(odd_part, 3, 0).reshape(K, 4 * BOXES, NH)
    tables = legendre.reshape(K, NH, L // 2, 2)

    def per_order(inputs):
        table_k, even_k, odd_k, order_id = inputs
        parity = order_id % 2
        first_src = jnp.where(parity == 0, even_k, odd_k)
        second = jnp.where(parity == 0, odd_k, even_k)
        low_half = jnp.dot(first_src, table_k[:, :, 0], preferred_element_type=jnp.float32)
        high_half = jnp.dot(second, table_k[:, :, 1], preferred_element_type=jnp.float32)
        return jnp.stack([low_half, high_half], axis=-1).reshape(4 * BOXES, L)

    result = lax.map(per_order, (tables, even_orders, odd_orders, jnp.arange(K, dtype=jnp.int32)))
    result = jnp.transpose(result.reshape(K, 4, BOXES, L), (1, 2, 3, 0))
    keep_mask = jnp.arange(L, dtype=jnp.int32)[None, :, None] < degree[:, None, None]
    kept = jnp.where(keep_mask[None], result, 0.0).astype(jnp.bfloat16)
    inverse = jnp.argsort(owner)
    return jnp.take(kept, inverse, axis=1)
```

```python
import functools
import math

import jax
import jax.numpy as jnp
import numpy as np
from jax import lax
from jax.experimental import pallas as pl
from jax.experimental.pallas import tpu as pltpu
from jax.sharding import PartitionSpec as P

MESH = pl.DeviceIdType.MESH
NTHETA, NPHI, NBOX = 8, 4, 8
CHUNKS = 4
PLANE = NTHETA * NPHI
ROWS = 128
COLS = 512
ORDERS = 16
BF = jnp.bfloat16
F32 = jnp.float32


def trig_table():
    total = NPHI * COLS
    orders = np.arange(PLANE * ORDERS).reshape(PLANE, 1, ORDERS, 1)
    angle = 2.0 * math.pi * (orders * np.arange(total) % total) / total
    table = np.concatenate([np.cos(angle), np.sin(angle)], axis=1)
    table = table.reshape(PLANE * 2 * ORDERS, NPHI, COLS).transpose(1, 0, 2)
    return np.ascontiguousarray(table).astype(jnp.bfloat16)


def dot(a, b):
    return jnp.dot(a, b, preferred_element_type=F32)


def dot_nt(a, b):
    return lax.dot_general(a, b, (((1,), (1,)), ((), ())), preferred_element_type=F32)


def iota(shape, dim):
    return lax.broadcasted_iota(jnp.int32, shape, dim)


def kernel(
    pattern, trig, table, degree, owner, out,
    pat, xsend, xrecv, trig_v, table_v, zsend, zrecv, lhs, prod, fsend, frecv,
    load_sem, xs_sem, xr_sem, zs_sem, zr_sem, fs_sem, fr_sem,
):
    me_t = lax.axis_index("theta")
    me_p = lax.axis_index("phi")
    me_b = lax.axis_index("box")

    def load(a):
        return pltpu.make_async_copy(pattern.at[a], pat.at[a], load_sem.at[a])

    for a in range(2):
        load(a).start()

    barrier = pltpu.get_barrier_semaphore()

    def greet_plane(r, carry):
        peer = ((me_t + r // NPHI) % NTHETA, (me_p + r % NPHI) % NPHI, me_b)
        pl.semaphore_signal(barrier, inc=1, device_id=peer, device_id_type=MESH)
        return carry

    def greet_boxes(r, carry):
        peer = ((me_t + r % NTHETA) % NTHETA, me_p, (me_b + r // NTHETA) % NBOX)
        pl.semaphore_signal(barrier, inc=1, device_id=peer, device_id_type=MESH)
        return carry

    lax.fori_loop(1, PLANE, greet_plane, 0)
    lax.fori_loop(NTHETA, NTHETA * NBOX, greet_boxes, 0)

    def box_of(slot):
        group = (me_b + slot + 1) % NBOX
        box = 0
        for b in range(8):
            box = jnp.where(owner[me_b * 8 + b] // 8 == group, b, box)
        return box

    boxes = [box_of(slot) for slot in range(8)]

    def cast(c):
        for half in range(2):
            for a in range(2):
                xsend[c, a * 2 + half] = pat[a, boxes[2 * c + half]].astype(BF)

    def send_x(c):
        for r in range(1, NPHI):
            dest = (me_p + r) % NPHI
            pltpu.make_async_remote_copy(
                src_ref=xsend.at[c, dest], dst_ref=xrecv.at[c, me_p],
                send_sem=xs_sem, recv_sem=xr_sem.at[c],
                device_id=(me_t, dest, me_b), device_id_type=MESH,
            ).start()
        pltpu.make_async_copy(xsend.at[c, me_p], xrecv.at[c, me_p], xr_sem.at[c]).start()

    def transform(c):
        pltpu.make_async_copy(xrecv.at[c], xrecv.at[c], xr_sem.at[c]).wait()

        def rows(m, carry):
            base = pl.multiple_of(m * 256, 256)
            acc = jnp.zeros((256, ROWS), F32)
            for s in range(NPHI):
                acc = acc + dot_nt(trig_v[s, pl.ds(base, 256), :], xrecv[c, s])
            zsend[c, pl.ds(m * 8, 8)] = acc.astype(BF).reshape(8, 2, ORDERS, ROWS)
            return carry

        lax.fori_loop(0, 4, rows, 0)

    def send_z(c):
        def one(r, carry):
            dt, dp = (me_t + r // NPHI) % NTHETA, (me_p + r % NPHI) % NPHI
            pltpu.make_async_remote_copy(
                src_ref=zsend.at[c, dp * NTHETA + dt], dst_ref=zrecv.at[c, me_t, me_p],
                send_sem=zs_sem, recv_sem=zr_sem.at[c],
                device_id=(dt, dp, me_b), device_id_type=MESH,
            ).start()
            return carry

        lax.fori_loop(1, PLANE, one, 0)
        pltpu.make_async_copy(
            zsend.at[c, me_p * NTHETA + me_t], zrecv.at[c, me_t, me_p], zr_sem.at[c]
        ).start()

    sq = (128, 128)
    gather_rows = (iota(sq, 1) == (iota(sq, 0) & 7) * 16 + (iota(sq, 0) >> 3)).astype(BF)
    spread_rows = (iota(sq, 0) == (iota(sq, 1) & 7) * 16 + (iota(sq, 1) >> 3)).astype(BF)
    reverse = (iota(sq, 0) + iota(sq, 1) == 127).astype(BF)
    identity = (iota(sq, 0) == iota(sq, 1)).astype(BF)

    def project(c):
        pltpu.make_async_copy(zrecv.at[c], zrecv.at[c], zr_sem.at[c]).wait()
        for i in range(4):
            north = zrecv[c, i].reshape(128, ROWS)
            south = zrecv[c, 7 - i].reshape(128, ROWS)
            south = dot(south, reverse).astype(BF)
            n_rows = dot(gather_rows, north).reshape(ORDERS, 8, ROWS)
            s_rows = dot(gather_rows, south).reshape(ORDERS, 8, ROWS)
            lhs[:, :, i * ROWS:(i + 1) * ROWS] = jnp.concatenate([n_rows, s_rows], axis=1).astype(BF)

        wide = (8, 512)
        lane, row = iota(wide, 1), iota(wide, 0)
        limit = jnp.where((row & 2) == 0, degree[boxes[2 * c]], degree[boxes[2 * c + 1]])
        keep = lane < limit
        straight = (iota((8, 128), 1) < 64) == (iota((8, 128), 0) < 4)

        def two_orders(h, carry):
            for odd in range(2):
                k = h * 2 + odd
                both = dot(lhs[k], table_v[k])
                north, south = both[:8], both[8:]
                value = jnp.where((lane & 1) == odd, north + south, north - south)
                value = jnp.where(keep, value, 0.0)
                for z in range(4):
                    v = value[:, z * 128:(z + 1) * 128]
                    w = pltpu.roll(pltpu.roll(v, 64, 1), 4, 0)
                    prod[z, pl.ds(pl.multiple_of(k * 8, 8), 8), :] = jnp.where(straight, v, w)
            return carry

        lax.fori_loop(0, ORDERS // 2, two_orders, 0)
        for z in range(4):
            block = dot(spread_rows, prod[z].astype(BF)).astype(BF)
            fsend[c, 2 * z:2 * z + 2] = block.reshape(2, 2, 2, ORDERS, 128)

    def send_f(c):
        def one(half, r):
            group = (me_b + 2 * c + half + 1) % NBOX
            dt = (me_t + r) % NTHETA
            return pltpu.make_async_remote_copy(
                src_ref=fsend.at[c, dt, half], dst_ref=frecv.at[me_b, me_t],
                send_sem=fs_sem, recv_sem=fr_sem,
                device_id=(dt, me_p, group), device_id_type=MESH,
            )

        for half in range(2):
            if (2 * c + half + 1) % NBOX:
                def go(r, carry):
                    one(half, r).start()
                    return carry
                lax.fori_loop(0, NTHETA, go, 0)
            else:
                def go_near(r, carry):
                    one(half, r).start()
                    return carry
                lax.fori_loop(1, NTHETA, go_near, 0)
                pltpu.make_async_copy(
                    fsend.at[c, me_t, half], frecv.at[me_b, me_t], fr_sem
                ).start()

    for a in range(2):
        load(a).wait()
    trig_load = pltpu.make_async_copy(trig, trig_v, load_sem.at[2])
    table_load = pltpu.make_async_copy(table.at[0], table_v, load_sem.at[3])
    trig_load.start()
    cast(0)
    pl.semaphore_wait(barrier, (PLANE - 1) + NTHETA * (NBOX - 1))
    send_x(0)
    cast(1)
    send_x(1)
    table_load.start()
    for c in range(2, CHUNKS):
        cast(c)
    trig_load.wait()
    for c in range(CHUNKS):
        transform(c)
        send_z(c)
        if c + 2 < CHUNKS:
            send_x(c + 2)
        if c == 1:
            table_load.wait()
        if c:
            project(c - 1)
            send_f(c - 1)
    project(CHUNKS - 1)
    send_f(CHUNKS - 1)

    def source_of(q):
        group = 0
        for b in range(64):
            group = jnp.where(owner[b] == me_b * 8 + q, b // 8, group)
        return group

    sources = [source_of(q) for q in range(8)]
    pltpu.make_async_copy(frecv, frecv, fr_sem).wait()
    for q in range(8):
        for s in range(2):
            block = frecv[sources[q], :, s].reshape(128, 128)
            turned = dot_nt(identity, block).astype(BF)
            out[2 * s, q] = turned[:64]
            out[2 * s + 1, q] = turned[64:]

    for c in range(CHUNKS):
        pltpu.make_async_copy(xsend.at[c, pl.ds(0, 3)], xsend.at[c, pl.ds(0, 3)], xs_sem).wait()
        pltpu.make_async_copy(zsend.at[c, pl.ds(0, 31)], zsend.at[c, pl.ds(0, 31)], zs_sem).wait()
    part = fsend.at[pl.ds(0, 3)]
    pltpu.make_async_copy(part, part, fs_sem).wait()
    part = fsend.at[3, pl.ds(0, 7)]
    pltpu.make_async_copy(part, part, fs_sem).wait()
    part = fsend.at[3, 7, 0]
    pltpu.make_async_copy(part, part, fs_sem).wait()


def local(pattern, legendre, degree, owner):
    any_space = pl.BlockSpec(memory_space=pl.ANY)
    smem = pl.BlockSpec(memory_space=pltpu.SMEM)
    vmem = pl.BlockSpec(memory_space=pltpu.VMEM)
    dma = pltpu.SemaphoreType.DMA
    return pl.pallas_call(
        kernel,
        out_shape=jax.ShapeDtypeStruct((4, 8, 64, 128), BF),
        in_specs=[any_space, any_space, any_space, smem, smem],
        out_specs=vmem,
        scratch_shapes=[
            pltpu.VMEM((2, 8, ROWS, COLS), F32),
            pltpu.VMEM((CHUNKS, NPHI, ROWS, COLS), BF),
            pltpu.VMEM((CHUNKS, NPHI, ROWS, COLS), BF),
            pltpu.VMEM((NPHI, PLANE * 2 * ORDERS, COLS), BF),
            pltpu.VMEM((ORDERS, 512, 512), BF),
            pltpu.VMEM((CHUNKS, PLANE, 2, ORDERS, ROWS), BF),
            pltpu.VMEM((CHUNKS, NTHETA, NPHI, 2, ORDERS, ROWS), BF),
            pltpu.VMEM((ORDERS, 16, 512), BF),
            pltpu.VMEM((4, 128, 128), F32),
            pltpu.VMEM((CHUNKS, NTHETA, 2, 2, ORDERS, 128), BF),
            pltpu.VMEM((NBOX, NTHETA, 2, ORDERS, 128), BF),
            dma((4,)), dma, dma((CHUNKS,)), dma, dma((CHUNKS,)), dma, dma,
        ],
        compiler_params=pltpu.CompilerParams(
            collective_id=0, has_side_effects=True, vmem_limit_bytes=48 * 1024 * 1024
        ),
        cost_estimate=pl.CostEstimate(
            flops=2_700_000_000, bytes_accessed=17_000_000, transcendentals=0
        ),
    )(pattern, jnp.asarray(trig_table()), legendre, degree, owner)


def solution(mesh):
    in_specs = (P(None, "box", "theta", "phi"), P("phi", "theta", None, None), P("box"), P())
    out_specs = P(None, "box", "theta", "phi")
    return jax.shard_map(local, mesh=mesh, in_specs=in_specs, out_specs=out_specs, check_vma=False)
```

```python
import functools
import math

import jax
import jax.numpy as jnp
import numpy as np
from jax import lax
from jax.experimental import pallas as pl
from jax.experimental.pallas import tpu as pltpu
from jax.sharding import PartitionSpec as P

MESH = pl.DeviceIdType.MESH
NTHETA, NPHI, NBOX = 8, 4, 8
CHUNKS = 4
PLANE = NTHETA * NPHI
ROWS = 128
COLS = 512
ORDERS = 16
BF = jnp.bfloat16
F32 = jnp.float32


def trig_table():
    total = NPHI * COLS
    orders = np.arange(PLANE * ORDERS).reshape(PLANE, 1, ORDERS, 1)
    angle = 2.0 * math.pi * (orders * np.arange(total) % total) / total
    table = np.concatenate([np.cos(angle), np.sin(angle)], axis=1)
    table = table.reshape(PLANE * 2 * ORDERS, NPHI, COLS).transpose(1, 0, 2)
    return np.ascontiguousarray(table).astype(jnp.bfloat16)


def dot(a, b):
    return jnp.dot(a, b, preferred_element_type=F32)


def dot_nt(a, b):
    return lax.dot_general(a, b, (((1,), (1,)), ((), ())), preferred_element_type=F32)


def iota(shape, dim):
    return lax.broadcasted_iota(jnp.int32, shape, dim)


def kernel(
    pattern, trig, table, degree, owner, out,
    pat, xsend, xrecv, trig_v, table_v, zsend, zrecv, lhs, prod, fsend, frecv, turned,
    load_sem, plane_sem, xs_sem, xr_sem, zs_sem, zr_sem, fs_sem, fr_sem,
):
    me_t = lax.axis_index("theta")
    me_p = lax.axis_index("phi")
    me_b = lax.axis_index("box")

    def load(a):
        return pltpu.make_async_copy(pattern.at[a], pat.at[a], load_sem.at[a])

    for a in range(2):
        load(a).start()

    barrier = pltpu.get_barrier_semaphore()

    def greet(semaphore, axis, size):
        mine = {"theta": me_t, "phi": me_p, "box": me_b}
        for r in range(1, size):
            peer = dict(mine)
            peer[axis] = (mine[axis] + r) % size
            pl.semaphore_signal(
                semaphore, inc=1, device_id=(peer["theta"], peer["phi"], peer["box"]),
                device_id_type=MESH,
            )

    greet(barrier, "phi", NPHI)
    greet(barrier, "theta", NTHETA)
    greet(barrier, "box", NBOX)

    def box_of(slot):
        group = (me_b + slot + 1) % NBOX
        box = 0
        for b in range(8):
            box = jnp.where(owner[me_b * 8 + b] // 8 == group, b, box)
        return box

    boxes = [box_of(slot) for slot in range(8)]

    def cast(c):
        for half in range(2):
            for a in range(2):
                xsend[c, a * 2 + half] = pat[a, boxes[2 * c + half]].astype(BF)

    def send_x(c):
        for r in range(1, NPHI):
            dest = (me_p + r) % NPHI
            pltpu.make_async_remote_copy(
                src_ref=xsend.at[c, dest], dst_ref=xrecv.at[c, me_p],
                send_sem=xs_sem, recv_sem=xr_sem.at[c],
                device_id=(me_t, dest, me_b), device_id_type=MESH,
            ).start()
        pltpu.make_async_copy(xsend.at[c, me_p], xrecv.at[c, me_p], xr_sem.at[c]).start()

    def transform(c):
        pltpu.make_async_copy(xrecv.at[c], xrecv.at[c], xr_sem.at[c]).wait()

        def group(g, carry):
            dp = (me_p + 1 + g) % NPHI
            base = pl.multiple_of(dp * 256, 256)
            acc = dot_nt(trig_v[0, pl.ds(base, 256), :], xrecv[c, 0])
            for s in range(1, NPHI):
                acc = acc + dot_nt(trig_v[s, pl.ds(base, 256), :], xrecv[c, s])
            zsend[c, pl.ds(dp * NTHETA, NTHETA)] = acc.astype(BF).reshape(NTHETA, 2, ORDERS, ROWS)
            if c == 0:
                @pl.when(g == 0)
                def _():
                    pl.semaphore_wait(plane_sem, NTHETA - 1)

            def one(r, carry):
                dt = (me_t + r) % NTHETA
                pltpu.make_async_remote_copy(
                    src_ref=zsend.at[c, dp * NTHETA + dt], dst_ref=zrecv.at[c, me_t, me_p],
                    send_sem=zs_sem, recv_sem=zr_sem.at[c],
                    device_id=(dt, dp, me_b), device_id_type=MESH,
                ).start()
                return carry

            lax.fori_loop(1, NTHETA, one, 0)

            @pl.when(g < NPHI - 1)
            def _():
                one(0, 0)
            return carry

        lax.fori_loop(0, NPHI, group, 0)
        pltpu.make_async_copy(
            zsend.at[c, me_p * NTHETA + me_t], zrecv.at[c, me_t, me_p], zr_sem.at[c]
        ).start()

    sq = (128, 128)
    gather_rows = (iota(sq, 1) == (iota(sq, 0) & 7) * 16 + (iota(sq, 0) >> 3)).astype(BF)
    spread_rows = (iota(sq, 0) == (iota(sq, 1) & 7) * 16 + (iota(sq, 1) >> 3)).astype(BF)
    reverse = (iota(sq, 0) + iota(sq, 1) == 127).astype(BF)
    identity = (iota(sq, 0) == iota(sq, 1)).astype(BF)

    def project(c):
        pltpu.make_async_copy(zrecv.at[c], zrecv.at[c], zr_sem.at[c]).wait()
        for i in range(4):
            north = zrecv[c, i].reshape(128, ROWS)
            south = zrecv[c, 7 - i].reshape(128, ROWS)
            south = dot(south, reverse).astype(BF)
            n_rows = dot(gather_rows, north).reshape(ORDERS, 8, ROWS)
            s_rows = dot(gather_rows, south).reshape(ORDERS, 8, ROWS)
            lhs[:, :, i * ROWS:(i + 1) * ROWS] = jnp.concatenate([n_rows, s_rows], axis=1).astype(BF)

        wide = (8, 256)
        lane, row = iota(wide, 1), iota(wide, 0)
        limit = jnp.where((row & 2) == 0, degree[boxes[2 * c]], degree[boxes[2 * c + 1]])
        straight = (iota((8, 128), 1) < 64) == (iota((8, 128), 0) < 4)

        for nh in range(2):
            def two_orders(h, carry):
                for odd in range(2):
                    k = h * 2 + odd
                    both = dot(lhs[k], table_v[k, :, nh * 256:(nh + 1) * 256])
                    north, south = both[:8], both[8:]
                    value = jnp.where((lane & 1) == odd, north + south, north - south)
                    value = jnp.where(lane + nh * 256 < limit, value, 0.0)
                    for z in range(2):
                        v = value[:, z * 128:(z + 1) * 128]
                        w = pltpu.roll(pltpu.roll(v, 64, 1), 4, 0)
                        at = pl.ds(pl.multiple_of(k * 8, 8), 8)
                        prod[nh * 2 + z, at, :] = jnp.where(straight, v, w)
                return carry

            lax.fori_loop(0, ORDERS // 2, two_orders, 0, unroll=True)
            for z in range(2 * nh, 2 * nh + 2):
                block = dot(spread_rows, prod[z].astype(BF)).astype(BF)
                fsend[c, 2 * z:2 * z + 2] = block.reshape(2, 2, 2, ORDERS, 128)
            for half in range(2):
                send_f(c, nh, half)

    def send_f(c, nh, half):
        group = (me_b + 2 * c + half + 1) % NBOX
        near = (2 * c + half + 1) % NBOX == 0

        def one(r, carry):
            dt = nh * 4 + (me_t + r) % 4
            def go():
                pltpu.make_async_remote_copy(
                    src_ref=fsend.at[c, dt, half], dst_ref=frecv.at[me_b, me_t],
                    send_sem=fs_sem, recv_sem=fr_sem.at[c],
                    device_id=(dt, me_p, group), device_id_type=MESH,
                ).start()
            if near:
                pl.when(dt != me_t)(go)
            else:
                go()
            return carry

        lax.fori_loop(0, 4, one, 0)
        if near and nh:
            pltpu.make_async_copy(fsend.at[c, me_t, half], frecv.at[me_b, me_t], fr_sem.at[c]).start()

    def finish(c):
        pltpu.make_async_copy(fsend.at[c], fsend.at[c], fr_sem.at[c]).wait()
        for half in range(2):
            slot = (2 * c + half + 1) % NBOX
            source = (me_b + NBOX - slot) % NBOX
            for s in range(2):
                block = frecv[source, :, s].reshape(128, 128)
                turned[slot, s] = dot_nt(identity, block).astype(BF)

    for a in range(2):
        load(a).wait()
    trig_load = pltpu.make_async_copy(trig, trig_v, load_sem.at[2])
    table_load = pltpu.make_async_copy(table.at[0], table_v, load_sem.at[3])
    trig_load.start()
    cast(0)
    pl.semaphore_wait(barrier, NPHI + NTHETA + NBOX - 3)
    send_x(0)
    greet(plane_sem, "theta", NTHETA)
    cast(1)
    send_x(1)
    table_load.start()
    for c in range(2, CHUNKS):
        cast(c)
    trig_load.wait()
    for c in range(CHUNKS):
        transform(c)
        if c + 2 < CHUNKS:
            send_x(c + 2)
        if c == 1:
            table_load.wait()
        if c:
            project(c - 1)
        if c > 1:
            finish(c - 2)
    project(CHUNKS - 1)
    finish(CHUNKS - 2)

    def source_of(q):
        group = 0
        for b in range(64):
            group = jnp.where(owner[b] == me_b * 8 + q, b // 8, group)
        return group

    slots = [(me_b + NBOX - source_of(q)) % NBOX for q in range(8)]
    finish(CHUNKS - 1)
    for q in range(8):
        for s in range(2):
            out[2 * s, q] = turned[slots[q], s, :64]
            out[2 * s + 1, q] = turned[slots[q], s, 64:]

    for c in range(CHUNKS):
        pltpu.make_async_copy(xsend.at[c, pl.ds(0, 3)], xsend.at[c, pl.ds(0, 3)], xs_sem).wait()
        pltpu.make_async_copy(zsend.at[c, pl.ds(0, 31)], zsend.at[c, pl.ds(0, 31)], zs_sem).wait()
    part = fsend.at[pl.ds(0, 3)]
    pltpu.make_async_copy(part, part, fs_sem).wait()
    part = fsend.at[3, pl.ds(0, 7)]
    pltpu.make_async_copy(part, part, fs_sem).wait()
    part = fsend.at[3, 7, 0]
    pltpu.make_async_copy(part, part, fs_sem).wait()


def local(pattern, legendre, degree, owner):
    any_space = pl.BlockSpec(memory_space=pl.ANY)
    smem = pl.BlockSpec(memory_space=pltpu.SMEM)
    vmem = pl.BlockSpec(memory_space=pltpu.VMEM)
    dma = pltpu.SemaphoreType.DMA
    return pl.pallas_call(
        kernel,
        out_shape=jax.ShapeDtypeStruct((4, 8, 64, 128), BF),
        in_specs=[any_space, any_space, any_space, smem, smem],
        out_specs=vmem,
        scratch_shapes=[
            pltpu.VMEM((2, 8, ROWS, COLS), F32),
            pltpu.VMEM((CHUNKS, NPHI, ROWS, COLS), BF),
            pltpu.VMEM((CHUNKS, NPHI, ROWS, COLS), BF),
            pltpu.VMEM((NPHI, PLANE * 2 * ORDERS, COLS), BF),
            pltpu.VMEM((ORDERS, 512, 512), BF),
            pltpu.VMEM((CHUNKS, PLANE, 2, ORDERS, ROWS), BF),
            pltpu.VMEM((CHUNKS, NTHETA, NPHI, 2, ORDERS, ROWS), BF),
            pltpu.VMEM((ORDERS, 16, 512), BF),
            pltpu.VMEM((4, 128, 128), F32),
            pltpu.VMEM((CHUNKS, NTHETA, 2, 2, ORDERS, 128), BF),
            pltpu.VMEM((NBOX, NTHETA, 2, ORDERS, 128), BF),
            pltpu.VMEM((NBOX, 2, 128, 128), BF),
            dma((4,)), pltpu.SemaphoreType.REGULAR,
            dma, dma((CHUNKS,)), dma, dma((CHUNKS,)), dma, dma((CHUNKS,)),
        ],
        compiler_params=pltpu.CompilerParams(
            collective_id=0, has_side_effects=True, vmem_limit_bytes=60 * 1024 * 1024
        ),
        cost_estimate=pl.CostEstimate(
            flops=2_700_000_000, bytes_accessed=17_000_000, transcendentals=0
        ),
    )(pattern, jnp.asarray(trig_table()), legendre, degree, owner)


def solution(mesh):
    in_specs = (P(None, "box", "theta", "phi"), P("phi", "theta", None, None), P("box"), P())
    out_specs = P(None, "box", "theta", "phi")
    return jax.shard_map(local, mesh=mesh, in_specs=in_specs, out_specs=out_specs, check_vma=False)
```

```python
import functools
import math

import jax
import jax.numpy as jnp
import numpy as np
from jax import lax
from jax.experimental import pallas as pl
from jax.experimental.pallas import tpu as pltpu
from jax.sharding import PartitionSpec as P

MESH = pl.DeviceIdType.MESH
NTHETA, NPHI, NBOX = 8, 4, 8
CHUNKS = 4
PLANE = NTHETA * NPHI
ROWS = 128
COLS = 512
ORDERS = 16
BF = jnp.bfloat16
F32 = jnp.float32


def trig_table():
    total = NPHI * COLS
    orders = np.arange(PLANE * ORDERS).reshape(PLANE, 1, ORDERS, 1)
    angle = 2.0 * math.pi * (orders * np.arange(total) % total) / total
    table = np.concatenate([np.cos(angle), np.sin(angle)], axis=1)
    table = table.reshape(PLANE * 2 * ORDERS, NPHI, COLS).transpose(1, 0, 2)
    return np.ascontiguousarray(table).astype(jnp.bfloat16)


def dot(a, b):
    return jnp.dot(a, b, preferred_element_type=F32)


def dot_nt(a, b):
    return lax.dot_general(a, b, (((1,), (1,)), ((), ())), preferred_element_type=F32)


def iota(shape, dim):
    return lax.broadcasted_iota(jnp.int32, shape, dim)


def kernel(
    pattern, trig, table, degree, owner, out,
    pat, xsend, xrecv, trig_v, table_v, zsend, zrecv, lhs, prod, fsend, frecv, turned,
    load_sem, plane_sem, xs_sem, xr_sem, zs_sem, zr_sem, fs_sem, fr_sem,
):
    me_t = lax.axis_index("theta")
    me_p = lax.axis_index("phi")
    me_b = lax.axis_index("box")

    def load(a):
        return pltpu.make_async_copy(pattern.at[a], pat.at[a], load_sem.at[a])

    for a in range(2):
        load(a).start()

    barrier = pltpu.get_barrier_semaphore()

    def greet(semaphore, axis, size):
        mine = {"theta": me_t, "phi": me_p, "box": me_b}
        for r in range(1, size):
            peer = dict(mine)
            peer[axis] = (mine[axis] + r) % size
            pl.semaphore_signal(
                semaphore, inc=1, device_id=(peer["theta"], peer["phi"], peer["box"]),
                device_id_type=MESH,
            )

    greet(barrier, "phi", NPHI)
    greet(barrier, "theta", NTHETA)
    greet(barrier, "box", NBOX)

    def box_of(slot):
        group = (me_b + slot + 1) % NBOX
        box = 0
        for b in range(8):
            box = jnp.where(owner[me_b * 8 + b] // 8 == group, b, box)
        return box

    boxes = [box_of(slot) for slot in range(8)]

    def cast(c):
        for half in range(2):
            for a in range(2):
                xsend[c, a * 2 + half] = pat[a, boxes[2 * c + half]].astype(BF)

    def send_x(c):
        for r in (2, 1, 3):
            dest = (me_p + r) % NPHI
            pltpu.make_async_remote_copy(
                src_ref=xsend.at[c, dest], dst_ref=xrecv.at[c, me_p],
                send_sem=xs_sem, recv_sem=xr_sem.at[c],
                device_id=(me_t, dest, me_b), device_id_type=MESH,
            ).start()
        pltpu.make_async_copy(xsend.at[c, me_p], xrecv.at[c, me_p], xr_sem.at[c]).start()

    def transform(c):
        pltpu.make_async_copy(xrecv.at[c], xrecv.at[c], xr_sem.at[c]).wait()

        def group(g, carry):
            dp = (me_p + 1 + g) % NPHI
            base = pl.multiple_of(dp * 256, 256)
            acc = dot_nt(trig_v[0, pl.ds(base, 256), :], xrecv[c, 0])
            for s in range(1, NPHI):
                acc = acc + dot_nt(trig_v[s, pl.ds(base, 256), :], xrecv[c, s])
            zsend[c, pl.ds(dp * NTHETA, NTHETA)] = acc.astype(BF).reshape(NTHETA, 2, ORDERS, ROWS)
            if c == 0:
                @pl.when(g == 0)
                def _():
                    pl.semaphore_wait(plane_sem, NTHETA - 1)

            def one(r, carry):
                dt = (me_t + r) % NTHETA
                pltpu.make_async_remote_copy(
                    src_ref=zsend.at[c, dp * NTHETA + dt], dst_ref=zrecv.at[c, me_t, me_p],
                    send_sem=zs_sem, recv_sem=zr_sem.at[c],
                    device_id=(dt, dp, me_b), device_id_type=MESH,
                ).start()
                return carry

            lax.fori_loop(1, NTHETA, one, 0)

            @pl.when(g < NPHI - 1)
            def _():
                one(0, 0)
            return carry

        lax.fori_loop(0, NPHI, group, 0)
        pltpu.make_async_copy(
            zsend.at[c, me_p * NTHETA + me_t], zrecv.at[c, me_t, me_p], zr_sem.at[c]
        ).start()

    sq = (128, 128)
    gather_rows = (iota(sq, 1) == (iota(sq, 0) & 7) * 16 + (iota(sq, 0) >> 3)).astype(BF)
    spread_rows = (iota(sq, 0) == (iota(sq, 1) & 7) * 16 + (iota(sq, 1) >> 3)).astype(BF)
    reverse = (iota(sq, 0) + iota(sq, 1) == 127).astype(BF)
    identity = (iota(sq, 0) == iota(sq, 1)).astype(BF)

    def project(c):
        pltpu.make_async_copy(zrecv.at[c], zrecv.at[c], zr_sem.at[c]).wait()
        if c + 3 < CHUNKS:
            send_x(c + 3)
        for i in range(4):
            north = zrecv[c, i].reshape(128, ROWS)
            south = zrecv[c, 7 - i].reshape(128, ROWS)
            south = dot(south, reverse).astype(BF)
            n_rows = dot(gather_rows, north).reshape(ORDERS, 8, ROWS)
            s_rows = dot(gather_rows, south).reshape(ORDERS, 8, ROWS)
            lhs[:, :, i * ROWS:(i + 1) * ROWS] = jnp.concatenate([n_rows, s_rows], axis=1).astype(BF)

        wide = (8, 256)
        lane, row = iota(wide, 1), iota(wide, 0)
        limit = jnp.where((row & 2) == 0, degree[boxes[2 * c]], degree[boxes[2 * c + 1]])
        straight = (iota((8, 128), 1) < 64) == (iota((8, 128), 0) < 4)

        for nh in range(2):
            def two_orders(h, carry):
                for odd in range(2):
                    k = h * 2 + odd
                    both = dot(lhs[k], table_v[k, :, nh * 256:(nh + 1) * 256])
                    north, south = both[:8], both[8:]
                    value = jnp.where((lane & 1) == odd, north + south, north - south)
                    value = jnp.where(lane + nh * 256 < limit, value, 0.0)
                    for z in range(2):
                        v = value[:, z * 128:(z + 1) * 128]
                        w = pltpu.roll(pltpu.roll(v, 64, 1), 4, 0)
                        at = pl.ds(pl.multiple_of(k * 8, 8), 8)
                        prod[nh * 2 + z, at, :] = jnp.where(straight, v, w)
                return carry

            lax.fori_loop(0, ORDERS // 2, two_orders, 0, unroll=True)
            for z in range(2 * nh, 2 * nh + 2):
                block = dot(spread_rows, prod[z].astype(BF)).astype(BF)
                fsend[c, 2 * z:2 * z + 2] = block.reshape(2, 2, 2, ORDERS, 128)
            for half in range(2):
                send_f(c, nh, half)

    def send_f(c, nh, half):
        group = (me_b + 2 * c + half + 1) % NBOX
        near = (2 * c + half + 1) % NBOX == 0

        def one(r, carry):
            dt = nh * 4 + (me_t + r) % 4
            def go():
                pltpu.make_async_remote_copy(
                    src_ref=fsend.at[c, dt, half], dst_ref=frecv.at[me_b, me_t],
                    send_sem=fs_sem, recv_sem=fr_sem.at[c],
                    device_id=(dt, me_p, group), device_id_type=MESH,
                ).start()
            if near:
                pl.when(dt != me_t)(go)
            else:
                go()
            return carry

        lax.fori_loop(0, 4, one, 0)
        if near and nh:
            pltpu.make_async_copy(fsend.at[c, me_t, half], frecv.at[me_b, me_t], fr_sem.at[c]).start()

    def finish(c):
        pltpu.make_async_copy(fsend.at[c], fsend.at[c], fr_sem.at[c]).wait()
        for half in range(2):
            slot = (2 * c + half + 1) % NBOX
            source = (me_b + NBOX - slot) % NBOX
            for s in range(2):
                block = frecv[source, :, s].reshape(128, 128)
                turned[slot, s] = dot_nt(identity, block).astype(BF)

    for a in range(2):
        load(a).wait()
    trig_load = pltpu.make_async_copy(trig, trig_v, load_sem.at[2])
    table_load = pltpu.make_async_copy(table.at[0], table_v, load_sem.at[3])
    trig_load.start()
    cast(0)
    pl.semaphore_wait(barrier, NPHI + NTHETA + NBOX - 3)
    send_x(0)
    greet(plane_sem, "theta", NTHETA)
    cast(1)
    send_x(1)
    table_load.start()
    for c in range(2, CHUNKS):
        cast(c)
    trig_load.wait()
    for c in range(CHUNKS):
        transform(c)
        if c == 0:
            send_x(2)
        if c == 1:
            table_load.wait()
        if c:
            project(c - 1)
        if c > 1:
            finish(c - 2)
    project(CHUNKS - 1)
    finish(CHUNKS - 2)

    def source_of(q):
        group = 0
        for b in range(64):
            group = jnp.where(owner[b] == me_b * 8 + q, b // 8, group)
        return group

    slots = [(me_b + NBOX - source_of(q)) % NBOX for q in range(8)]
    finish(CHUNKS - 1)
    for q in range(8):
        for s in range(2):
            out[2 * s, q] = turned[slots[q], s, :64]
            out[2 * s + 1, q] = turned[slots[q], s, 64:]

    for c in range(CHUNKS):
        pltpu.make_async_copy(xsend.at[c, pl.ds(0, 3)], xsend.at[c, pl.ds(0, 3)], xs_sem).wait()
        pltpu.make_async_copy(zsend.at[c, pl.ds(0, 31)], zsend.at[c, pl.ds(0, 31)], zs_sem).wait()
    part = fsend.at[pl.ds(0, 3)]
    pltpu.make_async_copy(part, part, fs_sem).wait()
    part = fsend.at[3, pl.ds(0, 7)]
    pltpu.make_async_copy(part, part, fs_sem).wait()
    part = fsend.at[3, 7, 0]
    pltpu.make_async_copy(part, part, fs_sem).wait()


def local(pattern, legendre, degree, owner):
    any_space = pl.BlockSpec(memory_space=pl.ANY)
    smem = pl.BlockSpec(memory_space=pltpu.SMEM)
    vmem = pl.BlockSpec(memory_space=pltpu.VMEM)
    dma = pltpu.SemaphoreType.DMA
    return pl.pallas_call(
        kernel,
        out_shape=jax.ShapeDtypeStruct((4, 8, 64, 128), BF),
        in_specs=[any_space, any_space, any_space, smem, smem],
        out_specs=vmem,
        scratch_shapes=[
            pltpu.VMEM((2, 8, ROWS, COLS), F32),
            pltpu.VMEM((CHUNKS, NPHI, ROWS, COLS), BF),
            pltpu.VMEM((CHUNKS, NPHI, ROWS, COLS), BF),
            pltpu.VMEM((NPHI, PLANE * 2 * ORDERS, COLS), BF),
            pltpu.VMEM((ORDERS, 512, 512), BF),
            pltpu.VMEM((CHUNKS, PLANE, 2, ORDERS, ROWS), BF),
            pltpu.VMEM((CHUNKS, NTHETA, NPHI, 2, ORDERS, ROWS), BF),
            pltpu.VMEM((ORDERS, 16, 512), BF),
            pltpu.VMEM((4, 128, 128), F32),
            pltpu.VMEM((CHUNKS, NTHETA, 2, 2, ORDERS, 128), BF),
            pltpu.VMEM((NBOX, NTHETA, 2, ORDERS, 128), BF),
            pltpu.VMEM((NBOX, 2, 128, 128), BF),
            dma((4,)), pltpu.SemaphoreType.REGULAR,
            dma, dma((CHUNKS,)), dma, dma((CHUNKS,)), dma, dma((CHUNKS,)),
        ],
        compiler_params=pltpu.CompilerParams(
            collective_id=0, has_side_effects=True, vmem_limit_bytes=60 * 1024 * 1024
        ),
        cost_estimate=pl.CostEstimate(
            flops=2_700_000_000, bytes_accessed=17_000_000, transcendentals=0
        ),
    )(pattern, jnp.asarray(trig_table()), legendre, degree, owner)


def solution(mesh):
    in_specs = (P(None, "box", "theta", "phi"), P("phi", "theta", None, None), P("box"), P())
    out_specs = P(None, "box", "theta", "phi")
    return jax.shard_map(local, mesh=mesh, in_specs=in_specs, out_specs=out_specs, check_vma=False)
```

```python
import functools
import math

import jax
import jax.numpy as jnp
import numpy as np
from jax import lax
from jax.experimental import pallas as pl
from jax.experimental.pallas import tpu as pltpu
from jax.sharding import PartitionSpec as P

MESH = pl.DeviceIdType.MESH
NTHETA, NPHI, NBOX = 8, 4, 8
CHUNKS = 4
PLANE = NTHETA * NPHI
ROWS = 128
COLS = 512
ORDERS = 16
BF = jnp.bfloat16
F32 = jnp.float32


def trig_table():
    total = NPHI * COLS
    orders = np.arange(PLANE * ORDERS).reshape(PLANE, 1, ORDERS, 1)
    angle = 2.0 * math.pi * (orders * np.arange(total) % total) / total
    table = np.concatenate([np.cos(angle), np.sin(angle)], axis=1)
    table = table.reshape(PLANE * 2 * ORDERS, NPHI, COLS).transpose(1, 0, 2)
    return np.ascontiguousarray(table).astype(jnp.bfloat16)


def dot(a, b):
    return jnp.dot(a, b, preferred_element_type=F32)


def dot_nt(a, b):
    return lax.dot_general(a, b, (((1,), (1,)), ((), ())), preferred_element_type=F32)


def iota(shape, dim):
    return lax.broadcasted_iota(jnp.int32, shape, dim)


def kernel(
    pattern, trig, table, degree, owner, out,
    pat, xsend, xrecv, trig_v, table_v, zsend, zrecv, lhs, prod, fsend, frecv, turned,
    load_sem, plane_sem, xs_sem, xr_sem, zs_sem, zr_sem, fs_sem, fr_sem,
):
    me_t = lax.axis_index("theta")
    me_p = lax.axis_index("phi")
    me_b = lax.axis_index("box")

    def load(a):
        return pltpu.make_async_copy(pattern.at[a], pat.at[a], load_sem.at[a])

    for a in range(2):
        load(a).start()

    barrier = pltpu.get_barrier_semaphore()

    def greet(semaphore, axis, size):
        mine = {"theta": me_t, "phi": me_p, "box": me_b}
        for r in range(1, size):
            peer = dict(mine)
            peer[axis] = (mine[axis] + r) % size
            pl.semaphore_signal(
                semaphore, inc=1, device_id=(peer["theta"], peer["phi"], peer["box"]),
                device_id_type=MESH,
            )

    greet(barrier, "phi", NPHI)
    greet(barrier, "theta", NTHETA)
    greet(barrier, "box", NBOX)

    def box_of(slot):
        group = (me_b + slot + 1) % NBOX
        box = 0
        for b in range(8):
            box = jnp.where(owner[me_b * 8 + b] // 8 == group, b, box)
        return box

    boxes = [box_of(slot) for slot in range(8)]

    def cast(c):
        for half in range(2):
            for a in range(2):
                xsend[c, a * 2 + half] = pat[a, boxes[2 * c + half]].astype(BF)

    def send_x(c):
        for r in (2, 1, 3):
            dest = (me_p + r) % NPHI
            pltpu.make_async_remote_copy(
                src_ref=xsend.at[c, dest], dst_ref=xrecv.at[c, me_p],
                send_sem=xs_sem, recv_sem=xr_sem.at[c],
                device_id=(me_t, dest, me_b), device_id_type=MESH,
            ).start()
        pltpu.make_async_copy(xsend.at[c, me_p], xrecv.at[c, me_p], xr_sem.at[c]).start()

    def transform(c):
        pltpu.make_async_copy(xrecv.at[c], xrecv.at[c], xr_sem.at[c]).wait()

        def group(g, carry):
            dp = (me_p + 1 + g) % NPHI
            base = pl.multiple_of(dp * 256, 256)
            acc = dot_nt(trig_v[0, pl.ds(base, 256), :], xrecv[c, 0])
            for s in range(1, NPHI):
                acc = acc + dot_nt(trig_v[s, pl.ds(base, 256), :], xrecv[c, s])
            zsend[c, pl.ds(dp * NTHETA, NTHETA)] = acc.astype(BF).reshape(NTHETA, 2, ORDERS, ROWS)
            if c == 0:
                @pl.when(g == 0)
                def _():
                    pl.semaphore_wait(plane_sem, NTHETA - 1)

            def one(r, carry):
                dt = (me_t + 3 + r) % NTHETA
                pltpu.make_async_remote_copy(
                    src_ref=zsend.at[c, dp * NTHETA + dt], dst_ref=zrecv.at[c, me_t, me_p],
                    send_sem=zs_sem, recv_sem=zr_sem.at[c],
                    device_id=(dt, dp, me_b), device_id_type=MESH,
                ).start()
                return carry

            lax.fori_loop(0, 5, one, 0)
            lax.fori_loop(6, NTHETA, one, 0)

            @pl.when(g < NPHI - 1)
            def _():
                one(5, 0)
            return carry

        lax.fori_loop(0, NPHI, group, 0)
        pltpu.make_async_copy(
            zsend.at[c, me_p * NTHETA + me_t], zrecv.at[c, me_t, me_p], zr_sem.at[c]
        ).start()

    sq = (128, 128)
    gather_rows = (iota(sq, 1) == (iota(sq, 0) & 7) * 16 + (iota(sq, 0) >> 3)).astype(BF)
    spread_rows = (iota(sq, 0) == (iota(sq, 1) & 7) * 16 + (iota(sq, 1) >> 3)).astype(BF)
    reverse = (iota(sq, 0) + iota(sq, 1) == 127).astype(BF)
    identity = (iota(sq, 0) == iota(sq, 1)).astype(BF)

    def project(c):
        pltpu.make_async_copy(zrecv.at[c], zrecv.at[c], zr_sem.at[c]).wait()
        if c + 3 < CHUNKS:
            send_x(c + 3)
        for i in range(4):
            north = zrecv[c, i].reshape(128, ROWS)
            south = zrecv[c, 7 - i].reshape(128, ROWS)
            south = dot(south, reverse).astype(BF)
            n_rows = dot(gather_rows, north).reshape(ORDERS, 8, ROWS)
            s_rows = dot(gather_rows, south).reshape(ORDERS, 8, ROWS)
            lhs[:, :, i * ROWS:(i + 1) * ROWS] = jnp.concatenate([n_rows, s_rows], axis=1).astype(BF)

        wide = (8, 256)
        lane, row = iota(wide, 1), iota(wide, 0)
        limit = jnp.where((row & 2) == 0, degree[boxes[2 * c]], degree[boxes[2 * c + 1]])
        straight = (iota((8, 128), 1) < 64) == (iota((8, 128), 0) < 4)

        for nh in range(2):
            def two_orders(h, carry):
                for odd in range(2):
                    k = h * 2 + odd
                    both = dot(lhs[k], table_v[k, :, nh * 256:(nh + 1) * 256])
                    north, south = both[:8], both[8:]
                    value = jnp.where((lane & 1) == odd, north + south, north - south)
                    value = jnp.where(lane + nh * 256 < limit, value, 0.0)
                    for z in range(2):
                        v = value[:, z * 128:(z + 1) * 128]
                        w = pltpu.roll(pltpu.roll(v, 64, 1), 4, 0)
                        at = pl.ds(pl.multiple_of(k * 8, 8), 8)
                        prod[nh * 2 + z, at, :] = jnp.where(straight, v, w)
                return carry

            lax.fori_loop(0, ORDERS // 2, two_orders, 0, unroll=True)
            for z in range(2 * nh, 2 * nh + 2):
                block = dot(spread_rows, prod[z].astype(BF)).astype(BF)
                fsend[c, 2 * z:2 * z + 2] = block.reshape(2, 2, 2, ORDERS, 128)
            for half in range(2):
                send_f(c, nh, half)

    def send_f(c, nh, half):
        group = (me_b + 2 * c + half + 1) % NBOX
        near = (2 * c + half + 1) % NBOX == 0

        def one(r, carry):
            dt = nh * 4 + (me_t + 2 + r) % 4
            def go():
                pltpu.make_async_remote_copy(
                    src_ref=fsend.at[c, dt, half], dst_ref=frecv.at[me_b, me_t],
                    send_sem=fs_sem, recv_sem=fr_sem.at[c],
                    device_id=(dt, me_p, group), device_id_type=MESH,
                ).start()
            if near:
                pl.when(dt != me_t)(go)
            else:
                go()
            return carry

        lax.fori_loop(0, 4, one, 0)
        if near and nh:
            pltpu.make_async_copy(fsend.at[c, me_t, half], frecv.at[me_b, me_t], fr_sem.at[c]).start()

    def finish(c):
        pltpu.make_async_copy(fsend.at[c], fsend.at[c], fr_sem.at[c]).wait()
        for half in range(2):
            slot = (2 * c + half + 1) % NBOX
            source = (me_b + NBOX - slot) % NBOX
            for s in range(2):
                block = frecv[source, :, s].reshape(128, 128)
                turned[slot, s] = dot_nt(identity, block).astype(BF)

    for a in range(2):
        load(a).wait()
    trig_load = pltpu.make_async_copy(trig, trig_v, load_sem.at[2])
    table_load = pltpu.make_async_copy(table.at[0], table_v, load_sem.at[3])
    trig_load.start()
    cast(0)
    pl.semaphore_wait(barrier, NPHI + NTHETA + NBOX - 3)
    send_x(0)
    greet(plane_sem, "theta", NTHETA)
    cast(1)
    send_x(1)
    table_load.start()
    for c in range(2, CHUNKS):
        cast(c)
    trig_load.wait()
    for c in range(CHUNKS):
        transform(c)
        if c == 0:
            send_x(2)
        if c == 1:
            table_load.wait()
        if c:
            project(c - 1)
        if c > 1:
            finish(c - 2)
    project(CHUNKS - 1)
    finish(CHUNKS - 2)

    def source_of(q):
        group = 0
        for b in range(64):
            group = jnp.where(owner[b] == me_b * 8 + q, b // 8, group)
        return group

    slots = [(me_b + NBOX - source_of(q)) % NBOX for q in range(8)]
    finish(CHUNKS - 1)
    for q in range(8):
        for s in range(2):
            out[2 * s, q] = turned[slots[q], s, :64]
            out[2 * s + 1, q] = turned[slots[q], s, 64:]

    for c in range(CHUNKS):
        pltpu.make_async_copy(xsend.at[c, pl.ds(0, 3)], xsend.at[c, pl.ds(0, 3)], xs_sem).wait()
        pltpu.make_async_copy(zsend.at[c, pl.ds(0, 31)], zsend.at[c, pl.ds(0, 31)], zs_sem).wait()
    part = fsend.at[pl.ds(0, 3)]
    pltpu.make_async_copy(part, part, fs_sem).wait()
    part = fsend.at[3, pl.ds(0, 7)]
    pltpu.make_async_copy(part, part, fs_sem).wait()
    part = fsend.at[3, 7, 0]
    pltpu.make_async_copy(part, part, fs_sem).wait()


def local(pattern, legendre, degree, owner):
    any_space = pl.BlockSpec(memory_space=pl.ANY)
    smem = pl.BlockSpec(memory_space=pltpu.SMEM)
    vmem = pl.BlockSpec(memory_space=pltpu.VMEM)
    dma = pltpu.SemaphoreType.DMA
    return pl.pallas_call(
        kernel,
        out_shape=jax.ShapeDtypeStruct((4, 8, 64, 128), BF),
        in_specs=[any_space, any_space, any_space, smem, smem],
        out_specs=vmem,
        scratch_shapes=[
            pltpu.VMEM((2, 8, ROWS, COLS), F32),
            pltpu.VMEM((CHUNKS, NPHI, ROWS, COLS), BF),
            pltpu.VMEM((CHUNKS, NPHI, ROWS, COLS), BF),
            pltpu.VMEM((NPHI, PLANE * 2 * ORDERS, COLS), BF),
            pltpu.VMEM((ORDERS, 512, 512), BF),
            pltpu.VMEM((CHUNKS, PLANE, 2, ORDERS, ROWS), BF),
            pltpu.VMEM((CHUNKS, NTHETA, NPHI, 2, ORDERS, ROWS), BF),
            pltpu.VMEM((ORDERS, 16, 512), BF),
            pltpu.VMEM((4, 128, 128), F32),
            pltpu.VMEM((CHUNKS, NTHETA, 2, 2, ORDERS, 128), BF),
            pltpu.VMEM((NBOX, NTHETA, 2, ORDERS, 128), BF),
            pltpu.VMEM((NBOX, 2, 128, 128), BF),
            dma((4,)), pltpu.SemaphoreType.REGULAR,
            dma, dma((CHUNKS,)), dma, dma((CHUNKS,)), dma, dma((CHUNKS,)),
        ],
        compiler_params=pltpu.CompilerParams(
            collective_id=0, has_side_effects=True, vmem_limit_bytes=60 * 1024 * 1024
        ),
        cost_estimate=pl.CostEstimate(
            flops=2_700_000_000, bytes_accessed=17_000_000, transcendentals=0
        ),
    )(pattern, jnp.asarray(trig_table()), legendre, degree, owner)


def solution(mesh):
    in_specs = (P(None, "box", "theta", "phi"), P("phi", "theta", None, None), P("box"), P())
    out_specs = P(None, "box", "theta", "phi")
    return jax.shard_map(local, mesh=mesh, in_specs=in_specs, out_specs=out_specs, check_vma=False)
```

```python
import functools
import math

import jax
import jax.numpy as jnp
import numpy as np
from jax import lax
from jax.experimental import pallas as pl
from jax.experimental.pallas import tpu as pltpu
from jax.sharding import PartitionSpec as P

MESH = pl.DeviceIdType.MESH
NTHETA, NPHI, NBOX = 8, 4, 8
CHUNKS = 4
PLANE = NTHETA * NPHI
ROWS = 128
COLS = 512
ORDERS = 16
BF = jnp.bfloat16
F32 = jnp.float32


def trig_table():
    total = NPHI * COLS
    orders = np.arange(PLANE * ORDERS).reshape(PLANE, 1, ORDERS, 1)
    angle = 2.0 * math.pi * (orders * np.arange(total) % total) / total
    table = np.concatenate([np.cos(angle), np.sin(angle)], axis=1)
    table = table.reshape(PLANE * 2 * ORDERS, NPHI, COLS).transpose(1, 0, 2)
    return np.ascontiguousarray(table).astype(jnp.bfloat16)


def dot(a, b):
    return jnp.dot(a, b, preferred_element_type=F32)


def dot_nt(a, b):
    return lax.dot_general(a, b, (((1,), (1,)), ((), ())), preferred_element_type=F32)


def iota(shape, dim):
    return lax.broadcasted_iota(jnp.int32, shape, dim)


def kernel(
    pattern, trig, table, degree, owner, out,
    pat, xsend, xrecv, trig_v, table_v, zsend, zrecv, lhs, prod, fsend, frecv, turned,
    load_sem, plane_sem, xs_sem, xr_sem, zs_sem, zr_sem, fs_sem, fr_sem,
):
    me_t = lax.axis_index("theta")
    me_p = lax.axis_index("phi")
    me_b = lax.axis_index("box")

    def load(a):
        return pltpu.make_async_copy(pattern.at[a], pat.at[a], load_sem.at[a])

    for a in range(2):
        load(a).start()

    barrier = pltpu.get_barrier_semaphore()

    def greet(semaphore, axis, size):
        mine = {"theta": me_t, "phi": me_p, "box": me_b}
        for r in range(1, size):
            peer = dict(mine)
            peer[axis] = (mine[axis] + r) % size
            pl.semaphore_signal(
                semaphore, inc=1, device_id=(peer["theta"], peer["phi"], peer["box"]),
                device_id_type=MESH,
            )

    greet(barrier, "phi", NPHI)
    greet(barrier, "theta", NTHETA)
    greet(barrier, "box", NBOX)

    def box_of(slot):
        group = (me_b + slot + 1) % NBOX
        box = 0
        for b in range(8):
            box = jnp.where(owner[me_b * 8 + b] // 8 == group, b, box)
        return box

    boxes = [box_of(slot) for slot in range(8)]

    def cast(c):
        for half in range(2):
            for a in range(2):
                xsend[c, a * 2 + half] = pat[a, boxes[2 * c + half]].astype(BF)

    def send_x(c):
        for r in (2, 1, 3):
            dest = (me_p + r) % NPHI
            pltpu.make_async_remote_copy(
                src_ref=xsend.at[c, dest], dst_ref=xrecv.at[c, me_p],
                send_sem=xs_sem, recv_sem=xr_sem.at[c],
                device_id=(me_t, dest, me_b), device_id_type=MESH,
            ).start()
        pltpu.make_async_copy(xsend.at[c, me_p], xrecv.at[c, me_p], xr_sem.at[c]).start()

    def transform(c):
        pltpu.make_async_copy(xrecv.at[c], xrecv.at[c], xr_sem.at[c]).wait()

        def group(g, carry):
            dp = (me_p + g) % NPHI
            base = pl.multiple_of(dp * 256, 256)
            acc = dot_nt(trig_v[0, pl.ds(base, 256), :], xrecv[c, 0])
            for s in range(1, NPHI):
                acc = acc + dot_nt(trig_v[s, pl.ds(base, 256), :], xrecv[c, s])
            zsend[c, pl.ds(dp * NTHETA, NTHETA)] = acc.astype(BF).reshape(NTHETA, 2, ORDERS, ROWS)
            if c == 0:
                @pl.when(g == 0)
                def _():
                    pl.semaphore_wait(plane_sem, NTHETA - 1)

            def one(r, carry):
                dt = (me_t + 3 + r) % NTHETA
                pltpu.make_async_remote_copy(
                    src_ref=zsend.at[c, dp * NTHETA + dt], dst_ref=zrecv.at[c, me_t, me_p],
                    send_sem=zs_sem, recv_sem=zr_sem.at[c],
                    device_id=(dt, dp, me_b), device_id_type=MESH,
                ).start()
                return carry

            lax.fori_loop(0, 5, one, 0)
            lax.fori_loop(6, NTHETA, one, 0)

            @pl.when(g > 0)
            def _():
                one(5, 0)
            return carry

        lax.fori_loop(0, NPHI, group, 0)
        pltpu.make_async_copy(
            zsend.at[c, me_p * NTHETA + me_t], zrecv.at[c, me_t, me_p], zr_sem.at[c]
        ).start()

    sq = (128, 128)
    gather_rows = (iota(sq, 1) == (iota(sq, 0) & 7) * 16 + (iota(sq, 0) >> 3)).astype(BF)
    spread_rows = (iota(sq, 0) == (iota(sq, 1) & 7) * 16 + (iota(sq, 1) >> 3)).astype(BF)
    reverse = (iota(sq, 0) + iota(sq, 1) == 127).astype(BF)
    identity = (iota(sq, 0) == iota(sq, 1)).astype(BF)

    def project(c):
        pltpu.make_async_copy(zrecv.at[c], zrecv.at[c], zr_sem.at[c]).wait()
        if c + 3 < CHUNKS:
            send_x(c + 3)
        for i in range(4):
            north = zrecv[c, i].reshape(128, ROWS)
            south = zrecv[c, 7 - i].reshape(128, ROWS)
            south = dot(south, reverse).astype(BF)
            n_rows = dot(gather_rows, north).reshape(ORDERS, 8, ROWS)
            s_rows = dot(gather_rows, south).reshape(ORDERS, 8, ROWS)
            lhs[:, :, i * ROWS:(i + 1) * ROWS] = jnp.concatenate([n_rows, s_rows], axis=1).astype(BF)

        wide = (8, 256)
        lane, row = iota(wide, 1), iota(wide, 0)
        limit = jnp.where((row & 2) == 0, degree[boxes[2 * c]], degree[boxes[2 * c + 1]])
        straight = (iota((8, 128), 1) < 64) == (iota((8, 128), 0) < 4)

        for nh in range(2):
            def two_orders(h, carry):
                for odd in range(2):
                    k = h * 2 + odd
                    both = dot(lhs[k], table_v[k, :, nh * 256:(nh + 1) * 256])
                    north, south = both[:8], both[8:]
                    value = jnp.where((lane & 1) == odd, north + south, north - south)
                    value = jnp.where(lane + nh * 256 < limit, value, 0.0)
                    for z in range(2):
                        v = value[:, z * 128:(z + 1) * 128]
                        w = pltpu.roll(pltpu.roll(v, 64, 1), 4, 0)
                        at = pl.ds(pl.multiple_of(k * 8, 8), 8)
                        prod[nh * 2 + z, at, :] = jnp.where(straight, v, w)
                return carry

            lax.fori_loop(0, ORDERS // 2, two_orders, 0, unroll=True)
            for z in range(2 * nh, 2 * nh + 2):
                block = dot(spread_rows, prod[z].astype(BF)).astype(BF)
                fsend[c, 2 * z:2 * z + 2] = block.reshape(2, 2, 2, ORDERS, 128)
            for half in range(2):
                send_f(c, nh, half)

    def send_f(c, nh, half):
        group = (me_b + 2 * c + half + 1) % NBOX
        near = (2 * c + half + 1) % NBOX == 0

        def one(r, carry):
            dt = nh * 4 + (me_t + 2 + r) % 4
            def go():
                pltpu.make_async_remote_copy(
                    src_ref=fsend.at[c, dt, half], dst_ref=frecv.at[me_b, me_t],
                    send_sem=fs_sem, recv_sem=fr_sem.at[c],
                    device_id=(dt, me_p, group), device_id_type=MESH,
                ).start()
            if near:
                pl.when(dt != me_t)(go)
            else:
                go()
            return carry

        lax.fori_loop(0, 4, one, 0)
        if near and nh:
            pltpu.make_async_copy(fsend.at[c, me_t, half], frecv.at[me_b, me_t], fr_sem.at[c]).start()

    def finish(c):
        pltpu.make_async_copy(fsend.at[c], fsend.at[c], fr_sem.at[c]).wait()
        for half in range(2):
            slot = (2 * c + half + 1) % NBOX
            source = (me_b + NBOX - slot) % NBOX
            for s in range(2):
                block = frecv[source, :, s].reshape(128, 128)
                turned[slot, s] = dot_nt(identity, block).astype(BF)

    for a in range(2):
        load(a).wait()
    trig_load = pltpu.make_async_copy(trig, trig_v, load_sem.at[2])
    table_load = pltpu.make_async_copy(table.at[0], table_v, load_sem.at[3])
    trig_load.start()
    cast(0)
    pl.semaphore_wait(barrier, NPHI + NTHETA + NBOX - 3)
    send_x(0)
    greet(plane_sem, "theta", NTHETA)
    cast(1)
    send_x(1)
    table_load.start()
    for c in range(2, CHUNKS):
        cast(c)
    trig_load.wait()
    for c in range(CHUNKS):
        transform(c)
        if c == 0:
            send_x(2)
        if c == 1:
            table_load.wait()
        if c:
            project(c - 1)
        if c > 1:
            finish(c - 2)
    project(CHUNKS - 1)
    finish(CHUNKS - 2)

    def source_of(q):
        group = 0
        for b in range(64):
            group = jnp.where(owner[b] == me_b * 8 + q, b // 8, group)
        return group

    slots = [(me_b + NBOX - source_of(q)) % NBOX for q in range(8)]
    finish(CHUNKS - 1)
    for q in range(8):
        for s in range(2):
            out[2 * s, q] = turned[slots[q], s, :64]
            out[2 * s + 1, q] = turned[slots[q], s, 64:]

    for c in range(CHUNKS):
        pltpu.make_async_copy(xsend.at[c, pl.ds(0, 3)], xsend.at[c, pl.ds(0, 3)], xs_sem).wait()
        pltpu.make_async_copy(zsend.at[c, pl.ds(0, 31)], zsend.at[c, pl.ds(0, 31)], zs_sem).wait()
    part = fsend.at[pl.ds(0, 3)]
    pltpu.make_async_copy(part, part, fs_sem).wait()
    part = fsend.at[3, pl.ds(0, 7)]
    pltpu.make_async_copy(part, part, fs_sem).wait()
    part = fsend.at[3, 7, 0]
    pltpu.make_async_copy(part, part, fs_sem).wait()


def local(pattern, legendre, degree, owner):
    any_space = pl.BlockSpec(memory_space=pl.ANY)
    smem = pl.BlockSpec(memory_space=pltpu.SMEM)
    vmem = pl.BlockSpec(memory_space=pltpu.VMEM)
    dma = pltpu.SemaphoreType.DMA
    return pl.pallas_call(
        kernel,
        out_shape=jax.ShapeDtypeStruct((4, 8, 64, 128), BF),
        in_specs=[any_space, any_space, any_space, smem, smem],
        out_specs=vmem,
        scratch_shapes=[
            pltpu.VMEM((2, 8, ROWS, COLS), F32),
            pltpu.VMEM((CHUNKS, NPHI, ROWS, COLS), BF),
            pltpu.VMEM((CHUNKS, NPHI, ROWS, COLS), BF),
            pltpu.VMEM((NPHI, PLANE * 2 * ORDERS, COLS), BF),
            pltpu.VMEM((ORDERS, 512, 512), BF),
            pltpu.VMEM((CHUNKS, PLANE, 2, ORDERS, ROWS), BF),
            pltpu.VMEM((CHUNKS, NTHETA, NPHI, 2, ORDERS, ROWS), BF),
            pltpu.VMEM((ORDERS, 16, 512), BF),
            pltpu.VMEM((4, 128, 128), F32),
            pltpu.VMEM((CHUNKS, NTHETA, 2, 2, ORDERS, 128), BF),
            pltpu.VMEM((NBOX, NTHETA, 2, ORDERS, 128), BF),
            pltpu.VMEM((NBOX, 2, 128, 128), BF),
            dma((4,)), pltpu.SemaphoreType.REGULAR,
            dma, dma((CHUNKS,)), dma, dma((CHUNKS,)), dma, dma((CHUNKS,)),
        ],
        compiler_params=pltpu.CompilerParams(
            collective_id=0, has_side_effects=True, vmem_limit_bytes=60 * 1024 * 1024
        ),
        cost_estimate=pl.CostEstimate(
            flops=2_700_000_000, bytes_accessed=17_000_000, transcendentals=0
        ),
    )(pattern, jnp.asarray(trig_table()), legendre, degree, owner)


def solution(mesh):
    in_specs = (P(None, "box", "theta", "phi"), P("phi", "theta", None, None), P("box"), P())
    out_specs = P(None, "box", "theta", "phi")
    return jax.shard_map(local, mesh=mesh, in_specs=in_specs, out_specs=out_specs, check_vma=False)
```
